32 devices in a mesh: elem: 8 (over z, x), span: 4 (over y, core).
Axes of the slice: x: 2, y: 2, z: 4, core: 2. Of those that a mesh axis runs over, the one named last changes fastest.
Arguments:
- adjoint: float32 [512, 5, 512], P(('span', 'elem')), may hold values from -6 to 6
- density: float32 [512], P(('span', 'elem')), may hold values from 0.5 to 2
- velocity: float32 [3, 512], P(None, ('span', 'elem')), may hold values from -1.2 to 1.2
- pressure: float32 [512], P(('span', 'elem')), may hold values from 0.4 to 1.6
- metric: float32 [3, 512], P(None, ('span', 'elem')), may hold values from 0.5 to 2
- face_source: int32 [32, 4], P('elem'), may hold values from 0 to 23, as said below
- face_flip: int32 [32, 4], P('elem'), may hold values from 0 to 1, as said below
- face_tag: int32 [32, 4], P('elem'), may hold values from 0 to 2, as said below
- send_list: int32 [32, 2], P('elem'), may hold values from 0 to 15, as said below
Outputs:
- adjoint_next: float32 [512, 5, 512], P(('span', 'elem'))
- register: float32 [512, 5, 512], P(('span', 'elem'))
The draws below stay inside these ranges and needn't reach their ends.
Inputs may be any that keep to these rules, and one draw needn't show every extreme that they name: `face_source`: on an interior face the value names the neighbouring face as in the reference program; neighbours lie on the same partition or on partitions at most two away, periodic over 8; the named face names this one back; each entry of a partition's four received blocks is named by at most one face. On tagged faces the value is the face's own number 4 c + f. Some partition uses all 2 entries of its blocks to the partitions one and two after it in every draw. `face_flip`: equal on the two faces of an interior pair; 0 on tagged faces. `face_tag`: 0 interior, 1 slip wall, 2 far field; every partition has a tagged face. `send_list`: row 4 p + r lists faces of partition p, numbered 4 c + f; the first n of them, with 1 <= n <= 2, are the faces whose neighbours lie on partition p + (1, 2, -1, -2)[r], in the order in which that partition names them; the rest are named by no face.
All inputs are finite; a program needn't handle non-finite values.
Results may differ from the reference program's by a relative error of at most 0.000068.
Values sent between devices are 32-bit elements; how exact they have to be, the bound alone decides.
No kernel may reach another device: no remote copies, remote signals or barrier semaphores. Data moves between devices by JAX's collectives and lax.ppermute only.
A program may use at most 64 MiB of HBM per device.

```python
import math
import jax
import jax.numpy as jnp
import numpy as np
from jax import lax

NV = 5
NODES = 512
COLS = 4
LAYERS = 4
SLOTS = 2
PARTS_SIZE = 8
ELEMS = 512
N_SPAN = 4


def build_tables(key):
    subkeys = jax.random.split(jax.random.fold_in(key, 11), 7)
    face_count = 4 * COLS
    partitions = jnp.arange(PARTS_SIZE, dtype=jnp.int32)
    counts = jax.random.randint(subkeys[0], (PARTS_SIZE, 2), (SLOTS + 1) // 2, SLOTS + 1)
    chosen = jax.random.randint(subkeys[1], (), 0, PARTS_SIZE)
    counts = jnp.where((partitions == chosen)[:, None], SLOTS, counts)
    region_counts = jnp.stack([counts[:, 0], counts[:, 1], jnp.roll(counts[:, 0], 1), jnp.roll(counts[:, 1], 2)], axis=1)
    orders = jax.vmap(lambda subkey: jax.random.permutation(subkey, face_count))(jax.random.split(subkeys[2], PARTS_SIZE)).astype(jnp.int32)
    pair_bits = jax.random.randint(subkeys[3], (PARTS_SIZE, 2, SLOTS), 0, 2)
    region_bits = jnp.stack([pair_bits[:, 0], pair_bits[:, 1], jnp.roll(pair_bits[:, 0], 1, axis=0), jnp.roll(pair_bits[:, 1], 2, axis=0)], axis=1)
    position = jnp.arange(face_count, dtype=jnp.int32)
    region = jnp.minimum(position // SLOTS, 3)
    within = position % SLOTS
    in_front = position < 4 * SLOTS
    is_remote = in_front[None, :] & (within[None, :] < region_counts[:, region])
    opposite = jnp.array([2, 3, 0, 1], dtype=jnp.int32)
    remote_source = 4 * COLS + opposite[region] * SLOTS + within
    remote_flip = region_bits[:, region, within]
    rest_flag = 1 - is_remote.astype(jnp.int32)
    ranking = jnp.cumsum(rest_flag, axis=1) - 1
    rest_total = jnp.sum(rest_flag, axis=1)
    border = jax.random.randint(subkeys[4], (PARTS_SIZE,), 1, COLS // 2 + 1)
    border = border + (rest_total - border) % 2
    rest_order = jnp.argsort(is_remote.astype(jnp.int32), axis=1, stable=True).astype(jnp.int32)
    mate_rank = jnp.bitwise_xor(ranking - border[:, None], 1) + border[:, None]
    mate_rank = jnp.clip(mate_rank, 0, face_count - 1)
    mate_position = jnp.take_along_axis(rest_order, mate_rank, axis=1)
    mate_slot = jnp.take_along_axis(orders, mate_position, axis=1)
    on_border = (rest_flag == 1) & (ranking < border[:, None])
    local_bits = jax.random.randint(subkeys[5], (PARTS_SIZE, face_count), 0, 2)
    local_flip = jnp.take_along_axis(local_bits, jnp.clip((ranking - border[:, None]) // 2, 0, face_count - 1), axis=1)
    border_tag = jax.random.randint(subkeys[6], (PARTS_SIZE, face_count), 1, 3)
    source_at = jnp.where(is_remote, remote_source[None, :], jnp.where(on_border, orders, mate_slot))
    flip_at = jnp.where(is_remote, remote_flip, jnp.where(on_border, 0, local_flip))
    tag_at = jnp.where(on_border, border_tag, 0)
    inverse = jnp.argsort(orders, axis=1).astype(jnp.int32)
    source_table = jnp.take_along_axis(source_at, inverse, axis=1).reshape(PARTS_SIZE * COLS, 4)
    flip_table = jnp.take_along_axis(flip_at, inverse, axis=1).reshape(PARTS_SIZE * COLS, 4)
    tag_table = jnp.take_along_axis(tag_at, inverse, axis=1).reshape(PARTS_SIZE * COLS, 4)
    send_table = orders[:, :4 * SLOTS].reshape(PARTS_SIZE * 4, SLOTS)
    return (source_table.astype(jnp.int32), flip_table.astype(jnp.int32), tag_table.astype(jnp.int32), send_table.astype(jnp.int32))


def draw_face_source(key, part):
    return build_tables(key)[0]


def draw_face_flip(key, part):
    return build_tables(key)[1]


def draw_face_tag(key, part):
    return build_tables(key)[2]


def draw_send_list(key, part):
    return build_tables(key)[3]


def block_levels(stream_key, extent, shards, least, top_value):
    factor_of = 1.0
    for dim, parts in shards:
        heights = jax.random.uniform(jax.random.fold_in(jax.random.fold_in(stream_key, 6), dim), (parts,), jnp.float32, least / len(shards), top_value / len(shards))
        factor_of = factor_of * jnp.repeat(jnp.exp(heights), extent[dim] // parts).reshape((-1,) + (1,) * (len(extent) - 1 - dim))
    return factor_of


def noise(key, dims, scale, bound, shards=(), held_as=jnp.bfloat16):
    entries = jax.random.normal(key, dims, jnp.float32) * scale
    if len(shards) > 0:
        entries = block_levels(key, dims, shards, -0.22, 0.18) * entries
    return jnp.clip(entries, min=-bound, max=bound).astype(held_as)


def setup_inputs(seed: int = 0) -> dict:
    arg_keys = jax.random.split(jax.random.key(seed), 10)
    adjoint = noise(arg_keys[0], (ELEMS, NV, NODES), 1.0, 6.0, ((0, 32),), jnp.float32)
    density = jnp.clip(jnp.exp(math.log(2.0) - 1.3862944 * jax.random.uniform(arg_keys[1], (ELEMS,), jnp.float32) ** block_levels(arg_keys[1], (ELEMS,), ((0, 32),), -0.2, 0.2)), 0.5, 2.0)
    velocity = noise(arg_keys[2], (3, ELEMS), 0.4, 1.2, ((1, 32),), jnp.float32)
    pressure = jnp.clip(jnp.exp(math.log(1.6) - 1.3862944 * jax.random.uniform(arg_keys[3], (ELEMS,), jnp.float32) ** block_levels(arg_keys[3], (ELEMS,), ((0, 32),), -0.2, 0.2)), 0.4, 1.6)
    metric = jnp.clip(jnp.exp(math.log(2.0) - 1.3862944 * jax.random.uniform(arg_keys[4], (3, ELEMS), jnp.float32) ** block_levels(arg_keys[4], (3, ELEMS), ((1, 32),), -0.2, 0.2)), 0.5, 2.0)
    face_source = draw_face_source(jax.random.fold_in(arg_keys[9], 71), 0)
    face_flip = draw_face_flip(jax.random.fold_in(arg_keys[9], 71), 0)
    face_tag = draw_face_tag(jax.random.fold_in(arg_keys[9], 71), 0)
    send_list = draw_send_list(jax.random.fold_in(arg_keys[9], 71), 0)
    return {"adjoint": adjoint, "density": density, "velocity": velocity, "pressure": pressure, "metric": metric, "face_source": face_source, "face_flip": face_flip, "face_tag": face_tag, "send_list": send_list}


gamma_gas = 1.4
lift_end = 28.0
time_step = 0.02
section_a2 = -567301805773.0 / 1357537059087.0
section_b1 = 1432997174477.0 / 9575080441755.0
section_b2 = 5161836677717.0 / 13612068292357.0

def lobatto_nodes():
    return [-1.0, -0.8717401485096066, -0.5917001814331423, -0.2092992179024789, 0.2092992179024789, 0.5917001814331423, 0.8717401485096066, 1.0]

def lobatto_derivative():
    positions = np.array(lobatto_nodes())
    total_nodes = positions.shape[0]
    differences = positions[:, None] - positions[None, :] + np.eye(total_nodes)
    weights = 1.0 / np.prod(differences, axis=1)
    matrix_out = weights[None, :] / weights[:, None] / differences
    matrix_out = matrix_out * (1.0 - np.eye(total_nodes))
    return matrix_out - np.eye(total_nodes) * np.sum(matrix_out, axis=1)[:, None]

def wall_table(columns):
    signs = np.ones((4, 5, 64))
    for face_index in range(4):
        signs[face_index, 1 + face_index // 2, :] = -1.0
    return np.tile(signs.reshape(4, 320), (columns, 1))

def adjoint_flux(values, direction, density_c, along, stiffness):
    components = [along * values[..., component, :] for component in range(5)]
    components[1 + direction] = components[1 + direction] + density_c * values[..., 0, :] + stiffness * values[..., 4, :]
    components[4] = components[4] + values[..., 1 + direction, :] / density_c
    return jnp.stack(components, axis=-2)

def volume_terms(derivatives, density_c, velocity_c, pressure_c, metric_c):
    stiffness = gamma_gas * pressure_c
    terms_list = [metric_c[direction][..., None] * adjoint_flux(derivatives[direction], direction, density_c, velocity_c[direction], stiffness) for direction in range(3)]
    return terms_list[0] + terms_list[1] + terms_list[2]

def face_terms(difference, density_c, velocity_c, pressure_c, metric_c):
    stiffness = gamma_gas * pressure_c
    sound = jnp.sqrt(stiffness / density_c)
    signs = jnp.concatenate([-jnp.ones((64,), jnp.float32), jnp.ones((64,), jnp.float32)])
    pieces = []
    for direction in range(3):
        block_in = difference[:, :, 128 * direction:128 * direction + 128]
        flux_out = adjoint_flux(block_in, direction, density_c, velocity_c[direction], stiffness)
        speed = jnp.abs(velocity_c[direction]) + sound
        pieces.append(0.5 * lift_end * metric_c[direction][..., None] * (signs * flux_out + speed[..., None] * block_in))
    return jnp.concatenate(pieces, axis=2)

def reference(adjoint, density, velocity, pressure, metric, face_source, face_flip, face_tag, send_list):
    span_layers = N_SPAN * LAYERS
    slab_columns = COLS * PARTS_SIZE
    face_total = 4 * COLS
    highest = lax.Precision.HIGHEST

    def to_layers(values):
        trailing = values.shape[1:]
        shaped = values.reshape((N_SPAN, PARTS_SIZE, LAYERS, COLS) + trailing)
        shaped = jnp.swapaxes(shaped, 1, 2)
        return shaped.reshape((span_layers, slab_columns) + trailing)

    def from_layers(values):
        trailing = values.shape[2:]
        shaped = values.reshape((N_SPAN, LAYERS, PARTS_SIZE, COLS) + trailing)
        shaped = jnp.swapaxes(shaped, 1, 2)
        return shaped.reshape((ELEMS,) + trailing)
    density_layers = to_layers(density)
    velocity_layers = to_layers(jnp.transpose(velocity))
    pressure_layers = to_layers(pressure)
    metric_layers = to_layers(jnp.transpose(metric))
    sources = face_source.reshape(PARTS_SIZE, face_total)
    partition = jnp.arange(PARTS_SIZE, dtype=jnp.int32)[:, None]
    remote = sources >= face_total
    region = jnp.where(remote, (sources - face_total) // SLOTS, 0).astype(jnp.int32)
    within = jnp.where(remote, (sources - face_total) % SLOTS, 0).astype(jnp.int32)
    offsets = jnp.array([1, 2, -1, -2], dtype=jnp.int32)
    sender = ((partition - offsets[region]) % PARTS_SIZE).astype(jnp.int32)
    send_rows = send_list.reshape(PARTS_SIZE, 4, SLOTS)
    partner_face = send_rows[sender, region, within]
    partner = jnp.where(remote, sender * face_total + partner_face, partition * face_total + sources).reshape(-1).astype(jnp.int32)
    flip_mask = (face_flip.reshape(-1) == 1)[None, :, None]
    tag_mask = face_tag.reshape(-1)[None, :, None]
    wall_sign = jnp.asarray(wall_table(slab_columns), jnp.float32)
    derivative = jnp.asarray(lobatto_derivative(), jnp.float32)

    def one_layer(inputs):
        layer_state, layer_difference, density_c, velocity_c, pressure_c, metric_c = inputs
        nodal_cube = layer_state.reshape(slab_columns, 5, 8, 8, 8)
        along_x = jnp.einsum('ip,nvkjp->nvkji', derivative, nodal_cube, precision=highest)
        along_y = jnp.einsum('jp,nvkpi->nvkji', derivative, nodal_cube, precision=highest)
        along_z = jnp.einsum('kp,nvpji->nvkji', derivative, nodal_cube, precision=highest)
        derivatives = [along_x.reshape(slab_columns, 5, 512), along_y.reshape(slab_columns, 5, 512), along_z.reshape(slab_columns, 5, 512)]
        density_col = density_c[:, None]
        velocity_col = [velocity_c[:, direction][:, None] for direction in range(3)]
        pressure_col = pressure_c[:, None]
        metric_col = [metric_c[:, direction][:, None] for direction in range(3)]
        volume = volume_terms(derivatives, density_col, velocity_col, pressure_col, metric_col)
        surface = face_terms(layer_difference, density_col, velocity_col, pressure_col, metric_col)
        pieces = [surface[:, :, 64 * face_index:64 * face_index + 64].reshape(slab_columns, 5, 8, 8) for face_index in range(6)]
        assembled = volume.reshape(slab_columns, 5, 8, 8, 8)
        assembled = assembled.at[:, :, :, :, 0].add(pieces[0])
        assembled = assembled.at[:, :, :, :, 7].add(pieces[1])
        assembled = assembled.at[:, :, :, 0, :].add(pieces[2])
        assembled = assembled.at[:, :, :, 7, :].add(pieces[3])
        assembled = assembled.at[:, :, 0].add(pieces[4])
        assembled = assembled.at[:, :, 7].add(pieces[5])
        return assembled.reshape(slab_columns, 5, 512)

    def residual(current):
        nodal_cube = current.reshape(span_layers, slab_columns, 5, 8, 8, 8)
        faces_list = [nodal_cube[..., 0], nodal_cube[..., 7], nodal_cube[..., 0, :], nodal_cube[..., 7, :], nodal_cube[:, :, :, 0], nodal_cube[:, :, :, 7]]
        traces = jnp.concatenate([face_block.reshape(span_layers, slab_columns, 5, 64) for face_block in faces_list], axis=3)
        in_plane = traces[..., :256].reshape(span_layers, slab_columns, 5, 4, 64)
        in_plane = jnp.swapaxes(in_plane, 2, 3).reshape(span_layers, 4 * slab_columns, 320)
        exterior = jnp.take(in_plane, partner, axis=1)
        mirrored = exterior.reshape(span_layers, 4 * slab_columns, 5, 8, 8)[..., ::-1].reshape(span_layers, 4 * slab_columns, 320)
        exterior = jnp.where(flip_mask, mirrored, exterior)
        exterior = jnp.where(tag_mask == 0, exterior, jnp.where(tag_mask == 1, in_plane * wall_sign, jnp.zeros_like(exterior)))
        outer_plane = jnp.swapaxes(exterior.reshape(span_layers, slab_columns, 4, 5, 64), 2, 3).reshape(span_layers, slab_columns, 5, 256)
        from_below = jnp.roll(traces[..., 320:], 1, axis=0)
        from_above = jnp.roll(traces[..., 256:320], -1, axis=0)
        difference = jnp.concatenate([outer_plane, from_below, from_above], axis=3) - traces
        return lax.map(one_layer, (current, difference, density_layers, velocity_layers, pressure_layers, metric_layers))
    start_state = to_layers(adjoint)
    section_one = time_step * residual(start_state)
    middle = start_state + section_b1 * section_one
    register = section_a2 * section_one + time_step * residual(middle)
    section_end = middle + section_b2 * register
    return (from_layers(section_end), from_layers(register))
```

```python
import functools

import jax
import jax.numpy as jnp
import numpy as np
from jax import lax
from jax.experimental import pallas as pl
from jax.experimental.pallas import tpu as pltpu
from jax.sharding import PartitionSpec as P

gamma_gas = 1.4
lift_end = 28.0
time_step = 0.02
section_a2 = -567301805773.0 / 1357537059087.0
section_b1 = 1432997174477.0 / 9575080441755.0
section_b2 = 5161836677717.0 / 13612068292357.0

LANES = 128
BLOCKS = 4
ROWS = 8
OFFSETS = (1, 2, -1, -2)


def passed_along(block, axis, distance):
    devices = range(lax.axis_size(axis))
    route = [((i - distance) % len(devices), i) for i in devices]
    return lax.ppermute(block, axis, route)


def lobatto_nodes():
    return [
        -1.0,
        -0.8717401485096066,
        -0.5917001814331423,
        -0.2092992179024789,
        0.2092992179024789,
        0.5917001814331423,
        0.8717401485096066,
        1.0,
    ]


def lobatto_derivative():
    positions = np.array(lobatto_nodes())
    total_nodes = positions.shape[0]
    differences = positions[:, None] - positions[None, :] + np.eye(total_nodes)
    weights = 1.0 / np.prod(differences, axis=1)
    matrix_out = weights[None, :] / weights[:, None] / differences
    matrix_out = matrix_out * (1.0 - np.eye(total_nodes))
    return matrix_out - np.eye(total_nodes) * np.sum(matrix_out, axis=1)[:, None]


def plane_tables():
    matrix_in = lobatto_derivative().astype(np.float32)
    along_x = np.kron(np.eye(16), matrix_in)
    along_y = np.kron(np.eye(2), np.kron(matrix_in, np.eye(8)))
    table = np.concatenate([along_x.T, along_y.T], axis=1).astype(np.float32)
    high = table.astype(jnp.bfloat16)
    low = (table - high.astype(np.float32)).astype(jnp.bfloat16)
    return high, low


def span_table():
    matrix_in = lobatto_derivative()
    rows = np.zeros((2, BLOCKS, BLOCKS, 2, 64))
    for swapped in range(2):
        for half in range(2):
            for out_block in range(BLOCKS):
                for in_block in range(BLOCKS):
                    rows[swapped, out_block, in_block, half] = matrix_in[
                        2 * out_block + half, 2 * in_block + (half ^ swapped)
                    ]
    return rows.reshape(2 * BLOCKS * BLOCKS, LANES).astype(np.float32)


def lane():
    return lax.broadcasted_iota(jnp.int32, (ROWS, LANES), 1)


def row_is(index):
    return lax.broadcasted_iota(jnp.int32, (ROWS, LANES), 0) == index


def lanes_of(values, index):
    return jnp.take_along_axis(values, index, axis=1, mode="promise_in_bounds")


def halves_swapped(values):
    return pltpu.roll(values, 64, 1)


def adjoint_flux(values, direction, factors):
    along, from_density, from_pressure, to_pressure = factors
    shape = values.shape
    return (
        along * values
        + from_density * jnp.broadcast_to(values[0:1], shape)
        + from_pressure * jnp.broadcast_to(values[4:5], shape)
        + to_pressure * jnp.broadcast_to(values[1 + direction : 2 + direction], shape)
    )


def flux_factors(flow, element, direction, scale):
    density, velocity, pressure, metric = flow
    zero = jnp.zeros((ROWS, LANES), jnp.float32)
    size = scale * metric[direction, element]
    rho = density[element]
    return (
        zero + size * velocity[direction, element],
        jnp.where(row_is(1 + direction), size * rho, 0.0),
        jnp.where(row_is(1 + direction), size * (gamma_gas * pressure[element]), 0.0),
        jnp.where(row_is(4), (zero + size) / (zero + rho), 0.0),
    )


def write_traces(blocks, column, layer, side_ref, span_ref):
    lanes = lane()
    second, k, a = lanes // 64, (lanes // 8) % 8, lanes % 8
    picks = (64 * (k % 2) + 8 * a + 7 * second, 64 * (k % 2) + 56 * second + a)
    for pair, pick in enumerate(picks):
        trace = lanes_of(blocks[0], pick)
        for block in range(1, BLOCKS):
            trace = jnp.where(k // 2 == block, lanes_of(blocks[block], pick), trace)
        side_ref[2 * column + pair, layer] = trace
    span_ref[layer, column] = jnp.where(lanes < 64, blocks[0], blocks[BLOCKS - 1])


def write_packets(send_list, side_ref, packet_refs):
    lanes = lane()
    for region, packet_ref in enumerate(packet_refs):
        faces = [send_list[region, slot] for slot in range(2)]
        picks = [lanes % 64 + 64 * (face % 2) for face in faces]
        for layer in range(packet_ref.shape[0]):
            parts = [lanes_of(side_ref[face // 2, layer], pick) for face, pick in zip(faces, picks)]
            packet_ref[layer] = jnp.where(lanes < 64, parts[0], parts[1])


def first_traces(layers, columns, send_list, adjoint_ref, state_ref, side_ref, span_ref, *packet_refs):
    padding = jnp.zeros((ROWS - adjoint_ref.shape[1], LANES), jnp.float32)

    @pl.loop(0, columns)
    def _(column):
        for layer in range(layers):
            element = layer * columns + column
            blocks = []
            for block in range(BLOCKS):
                at = pl.ds(block * LANES, LANES)
                blocks.append(jnp.concatenate([adjoint_ref[element, :, at], padding], axis=0))
                state_ref[element, :, at] = blocks[-1]
            write_traces(blocks, column, layer, side_ref, span_ref)

    write_packets(send_list, side_ref, packet_refs)


def volume_terms(
    layers, columns, carry_scale, density, velocity, pressure, metric, *refs
):
    if carry_scale is None:
        state_ref, high_ref, low_ref, factor_ref, out_ref, plane_ref = refs
    else:
        state_ref, high_ref, low_ref, factor_ref, carried_ref, out_ref, plane_ref = refs
    flow = (density, velocity, pressure, metric)
    elements = layers * columns
    for block in range(BLOCKS):
        values = state_ref[:, :, pl.ds(block * LANES, LANES)].reshape(elements * ROWS, LANES)
        high = values.astype(jnp.bfloat16)
        low = (values - high.astype(jnp.float32)).astype(jnp.bfloat16)
        product = functools.partial(jnp.dot, preferred_element_type=jnp.float32)
        plane_ref[block] = (
            product(high, high_ref[...]) + product(high, low_ref[...]) + product(low, high_ref[...])
        ).reshape(elements, ROWS, 2 * LANES)

    @pl.loop(0, elements)
    def _(element):
        factors = [flux_factors(flow, element, direction, time_step) for direction in range(3)]
        blocks = [state_ref[element, :, pl.ds(block * LANES, LANES)] for block in range(BLOCKS)]
        swapped = [halves_swapped(values) for values in blocks]
        for block in range(BLOCKS):
            at = pl.ds(block * LANES, LANES)
            total = adjoint_flux(plane_ref[block, element, :, pl.ds(0, LANES)], 0, factors[0])
            total += adjoint_flux(plane_ref[block, element, :, pl.ds(LANES, LANES)], 1, factors[1])
            along_z = jnp.zeros((ROWS, LANES), jnp.float32)
            for source in range(BLOCKS):
                row = BLOCKS * block + source
                along_z += factor_ref[pl.ds(row, 1), :] * blocks[source]
                along_z += factor_ref[pl.ds(BLOCKS * BLOCKS + row, 1), :] * swapped[source]
            total += adjoint_flux(along_z, 2, factors[2])
            if carry_scale is not None:
                total += carry_scale * carried_ref[element, :, at]
            out_ref[element, :, at] = total


def surface_terms(layers, columns, flow, tables, own, arrived, sources_ref, emit):
    face_source, face_flip, face_tag = tables
    side_ref, span_ref = own
    *packet_refs, below_ref, above_ref = arrived
    pairs = 2 * columns
    sources_ref[pl.ds(0, pairs)] = side_ref[...]
    for region, packet_ref in enumerate(packet_refs):
        sources_ref[pairs + region] = packet_ref[...]

    @pl.loop(0, columns)
    def _(column):
        lanes = lane()
        first = lanes < 64
        i, j, k_half = lanes % 8, (lanes // 8) % 8, lanes // 64
        sign = jnp.where(first, -1.0, 1.0)
        zero = jnp.zeros((ROWS, LANES), jnp.float32)
        sides = []
        for pair in range(2):
            faces = []
            for face in (2 * pair, 2 * pair + 1):
                source = face_source[column, face]
                tag = face_tag[column, face]
                pick = (lanes % 64) ^ (7 * face_flip[column, face])
                pick = pick + 64 * (source % 2)
                inside = jnp.where(tag == 0, 1.0, 0.0)
                wall = jnp.where(tag == 1, 1.0, 0.0)
                kept = jnp.where(row_is(1 + pair), -1.0 - wall, wall - 1.0)
                faces.append((source // 2, pick, zero + inside, kept))
            pick = jnp.where(first, faces[0][1], faces[1][1])
            inside = jnp.where(first, faces[0][2], faces[1][2])
            kept = jnp.where(first, faces[0][3], faces[1][3])
            sides.append((faces[0][0], faces[1][0], pick, inside, kept))
        for layer in range(layers):
            element = layer * columns + column
            differences = []
            for pair, (one, two, pick, inside, kept) in enumerate(sides):
                exterior = jnp.where(
                    first,
                    lanes_of(sources_ref[one, layer], pick),
                    lanes_of(sources_ref[two, layer], pick),
                )
                differences.append(inside * exterior + kept * side_ref[2 * column + pair, layer])
            below = below_ref[column] if layer == 0 else span_ref[layer - 1, column]
            above = above_ref[column] if layer == layers - 1 else span_ref[layer + 1, column]
            differences.append(
                halves_swapped(jnp.where(first, above, below)) - span_ref[layer, column]
            )
            lifts = []
            density, velocity, pressure, metric = flow
            sound = jnp.sqrt((zero + gamma_gas * pressure[element]) / (zero + density[element]))
            for direction, difference in enumerate(differences):
                scale = 0.5 * lift_end * time_step
                factors = flux_factors(flow, element, direction, scale)
                speed = (scale * metric[direction, element]) * (
                    sound + jnp.abs(velocity[direction, element])
                )
                lifts.append(
                    sign * adjoint_flux(difference, direction, factors) + speed * difference
                )
            total = []
            for block in range(BLOCKS):
                k = 2 * block + k_half
                on_x = lanes_of(lifts[0], jnp.where(i == 7, 64, 0) + 8 * k + j)
                on_y = lanes_of(lifts[1], jnp.where(j == 7, 64, 0) + 8 * k + i)
                lift = jnp.where((i == 0) | (i == 7), on_x, 0.0)
                lift += jnp.where((j == 0) | (j == 7), on_y, 0.0)
                if block == 0:
                    lift += jnp.where(first, lifts[2], 0.0)
                if block == BLOCKS - 1:
                    lift += jnp.where(first, 0.0, lifts[2])
                total.append(lift)
            emit(element, column, layer, total)


def first_section(layers, columns, *refs):
    flow, tables, send_list, refs = refs[:4], refs[4:7], refs[7], refs[8:]
    state_ref, volume_ref, own, arrived, refs = refs[0], refs[1], refs[2:4], refs[4:10], refs[10:]
    section_ref, middle_ref, side_ref, span_ref, *packet_refs, sources_ref = refs

    def emit(element, column, layer, lift):
        blocks = []
        for block in range(BLOCKS):
            at = pl.ds(block * LANES, LANES)
            section = volume_ref[element, :, at] + lift[block]
            section_ref[element, :, at] = section
            blocks.append(state_ref[element, :, at] + section_b1 * section)
            middle_ref[element, :, at] = blocks[-1]
        write_traces(blocks, column, layer, side_ref, span_ref)

    surface_terms(layers, columns, flow, tables, own, arrived, sources_ref, emit)
    write_packets(send_list, side_ref, packet_refs)


def second_section(layers, columns, *refs):
    flow, tables, refs = refs[:4], refs[4:7], refs[7:]
    middle_ref, volume_ref, own, arrived, refs = refs[0], refs[1], refs[2:4], refs[4:10], refs[10:]
    next_ref, register_ref, sources_ref = refs
    variables = next_ref.shape[1]

    def emit(element, column, layer, lift):
        for block in range(BLOCKS):
            at = pl.ds(block * LANES, LANES)
            register = volume_ref[element, :, at] + lift[block]
            result = middle_ref[element, :, at] + section_b2 * register
            register_ref[element, :, at] = register[:variables]
            next_ref[element, :, at] = result[:variables]

    surface_terms(layers, columns, flow, tables, own, arrived, sources_ref, emit)


def in_vmem(*shape):
    return pltpu.VMEM(shape, jnp.float32)


def on_device(
    adjoint, density, velocity, pressure, metric, face_source, face_flip, face_tag, send_list
):
    elements, variables, nodes = adjoint.shape
    columns = face_source.shape[0]
    layers = elements // columns
    flow = (density, velocity, pressure, metric)
    tables = (face_source, face_flip, face_tag)
    state_like = in_vmem(elements, ROWS, nodes)
    side_like = in_vmem(2 * columns, layers, ROWS, LANES)
    span_like = in_vmem(layers, columns, ROWS, LANES)
    packets_like = [in_vmem(layers, ROWS, LANES)] * len(OFFSETS)
    sources_like = pltpu.VMEM((2 * columns + len(OFFSETS), layers, ROWS, LANES), jnp.float32)
    smem = pl.BlockSpec(memory_space=pltpu.SMEM)
    vmem = pl.BlockSpec(memory_space=pltpu.VMEM)

    def call(kernel, scalars, arrays, outs, scratch=()):
        return pl.pallas_call(
            functools.partial(kernel, layers, columns),
            in_specs=[smem] * len(scalars) + [vmem] * len(arrays),
            out_specs=[vmem] * len(outs),
            out_shape=outs,
            scratch_shapes=list(scratch),
            cost_estimate=pl.CostEstimate(flops=2000000, bytes_accessed=1000000, transcendentals=0),
            compiler_params=pltpu.CompilerParams(vmem_limit_bytes=24 * 1024 * 1024),
        )(*scalars, *arrays)

    def exchanged(span_traces, packets):
        arrived = [
            passed_along(packet, "elem", offset) for packet, offset in zip(packets, OFFSETS)
        ]
        below = passed_along(span_traces[layers - 1], "span", 1)
        above = passed_along(span_traces[0], "span", -1)
        return (*arrived, below, above)

    state, side, span, *packets = call(
        first_traces, (send_list,), (adjoint,), [state_like, side_like, span_like, *packets_like]
    )
    constants = tuple(jnp.asarray(table) for table in (*plane_tables(), span_table()))
    plane_like = pltpu.VMEM((BLOCKS, elements, ROWS, 2 * LANES), jnp.float32)
    arrived = exchanged(span, packets)
    (volume,) = call(
        functools.partial(with_carry, None), flow, (state, *constants), [state_like], [plane_like]
    )
    section, middle, side, span, *packets = call(
        first_section,
        (*flow, *tables, send_list),
        (state, volume, side, span, *arrived),
        [state_like, state_like, side_like, span_like, *packets_like],
        [sources_like],
    )
    arrived = exchanged(span, packets)
    (volume,) = call(
        functools.partial(with_carry, section_a2),
        flow,
        (middle, *constants, section),
        [state_like],
        [plane_like],
    )
    out_like = jax.ShapeDtypeStruct(adjoint.shape, adjoint.dtype)
    return tuple(
        call(
            second_section,
            (*flow, *tables),
            (middle, volume, side, span, *arrived),
            [out_like, out_like],
            [sources_like],
        )
    )


def with_carry(carry_scale, layers, columns, *refs):
    volume_terms(layers, columns, carry_scale, *refs)


def solution(mesh):
    placed = (
        P(("span", "elem"), None, None),
        P(("span", "elem")),
        P(None, ("span", "elem")),
        P(("span", "elem")),
        P(None, ("span", "elem")),
        P("elem", None),
        P("elem", None),
        P("elem", None),
        P("elem", None),
    )
    return jax.shard_map(
        on_device,
        mesh=mesh,
        in_specs=placed,
        out_specs=(P(("span", "elem"), None, None), P(("span", "elem"), None, None)),
        check_vma=False,
    )
```
